768 devices in a mesh: row: 24 (over z, y_lo), col: 32 (over x, y_hi, core).
Axes of the slice: x: 4, y: 8 (y_hi: 4, y_lo: 2; y = y_hi * 2 + y_lo), z: 12, core: 2. Of those that a mesh axis runs over, the one named last changes fastest.
Arguments:
- density_panel: bfloat16 [12288, 98304], P('row', 'col'), may hold values from -6 to 6
- density_pattern: int32 [96, 768], P('row', 'col'), may hold values 0 or 1
- margin_blocks: bfloat16 [24, 1024, 128, 128], P('row', 'col'), may hold values from -0.3125 to 0.3125
- margin_owner: int32 [24, 1024, 1], P('row', 'col'), may hold values from 0 to 31; in each aligned block of 32 rows (0 to 31, 32 to 63, ..., all dimensions but the last counted through in order) at most 2 rows name the same one
- margin_place: int32 [24, 1024], P('row', 'col'), may hold values from 0 to 63
Outputs:
- product_panel: float32 [12288, 8192], P('row', 'col')
The draws below stay inside these ranges and needn't reach their ends.
Inputs may be any that keep to these rules, and one draw needn't show every extreme that they name: `margin_owner`: among the 32 blocks of one device no owner is named more than 2 times.
All inputs are finite; a program needn't handle non-finite values. No bound on the sum of `density_pattern` on one device may be relied on, other than what follows from the above.
Results may differ from the reference program's by a relative error of at most 0.002.
Values may be sent and summed in bfloat16 or wider, within the bound.
A program may use at most 64 MiB of HBM per device.

```python
import math
import jax
import jax.numpy as jnp
import numpy as np
from jax import lax

BS = 128
RB = 4
KB = 1
CB = 2
CAP = 2
SECTIONS = 3
NS = 32
GROUPS = 768
ROWS = 12288
INNER = 98304
N_ROW = 24
N_COL = 32


def plant(entries, stream_key, smallest, largest):
    longest = entries.shape.index(max(entries.shape))
    spots = []
    for shift in (0, 1):
        where = [jax.random.randint(jax.random.fold_in(stream_key, axis), (), 0, length) for axis, length in enumerate(entries.shape)]
        where[longest] = (where[longest] + shift) % entries.shape[longest]
        spots.append(tuple(where))
    return entries.at[spots[0]].set(smallest).at[spots[1]].set(largest)


def level_of(stream_key, extent, split, low, high):
    def one(dim, parts):
        steps = jax.random.uniform(jax.random.fold_in(jax.random.fold_in(stream_key, 6), dim), (parts,), jnp.float32, low / len(split), high / len(split))
        return jnp.repeat(jnp.exp(steps), extent[dim] // parts).reshape((-1,) + (1,) * (len(extent) - dim - 1))

    level = one(*split[0])
    for cut in split[1:]:
        level = level * one(*cut)
    return level


def shared_out(own_key, own, number, rows, amount, top, most, skew):
    ranking = jax.random.permutation(own_key, amount)
    heavy_load, ordinary = load_shares(amount, rows * top, most, skew, True), load_shares(amount, rows * top, most, skew, False)
    places = jnp.arange(amount)

    def named(tallies, rotation):
        used = int((tallies > 0).sum())
        fixed = max(1, used // 4)
        moved = fixed + (places - fixed + rotation * (used - fixed)) % max(1, amount - fixed)
        return jnp.zeros((amount,), jnp.int32).at[ranking[jnp.where(places < fixed, places, moved)]].set(jnp.asarray(tallies, jnp.int32))

    tallies = jnp.where(number % 4 == 0, named(heavy_load, number // 4), named(ordinary, number - number // 4 - 1))
    mixed = jax.random.permutation(jax.random.fold_in(own, 3), amount)
    giver, receiver = mixed[0:amount // 2 * 2:2], mixed[1:amount // 2 * 2:2]
    slack = jnp.minimum(tallies[giver] - 1, most - tallies[receiver]) // 2
    slack = jnp.where((giver == ranking[0]) | (receiver == ranking[0]) | (tallies[receiver] == 0), 0, jnp.maximum(slack, 0))
    moved = jax.random.randint(jax.random.fold_in(own, 4), (amount // 2,), 0, 1 << 20) % (slack + 1)
    tallies = tallies.at[giver].add(-moved).at[receiver].add(moved)
    items = jnp.searchsorted(jnp.cumsum(tallies), jnp.arange(rows * top), side="right").astype(jnp.int32)
    listing = items.reshape(top, rows).T
    listing = listing[jax.random.permutation(jax.random.fold_in(own, 1), rows)]
    rotation = jax.random.randint(jax.random.fold_in(own, 2), (rows, 1), 0, top)
    return jnp.take_along_axis(listing, (jnp.arange(top)[None, :] + rotation) % top, axis=1)


def load_shares(number_of, total, limit, lean, full):
    weights = [(1 << 20) // math.isqrt(rank ** lean) + 1 for rank in range(1, number_of + 1)]
    largest = limit if full else min(limit, max(-(-total // number_of), total * weights[0] // sum(weights)))
    least = 1 if total - largest >= number_of - 1 else 0
    given, spare = [largest] + [least] * (number_of - 1), total - largest - least * (number_of - 1)
    while spare > 0:
        candidates = [i for i in range(1, number_of) if given[i] < largest] or [i for i in range(1, number_of) if given[i] < limit]
        whole, remaining = sum([weights[i] for i in candidates]), spare
        for i in candidates:
            addition = min(limit - given[i], max(1, remaining * weights[i] // whole), spare)
            given[i] = given[i] + addition
            spare = spare - addition
    return np.array(given)


def normal_values(own_key, extent, scale, reach, split=(), kind=jnp.bfloat16):
    level = level_of(own_key, extent, split, -0.22, 0.18) if split else 1.0
    array = jax.random.normal(own_key, extent, jnp.float32) * scale * level
    return jnp.minimum(jnp.maximum(array, -reach), reach).astype(kind)


def setup_inputs(seed: int = 0) -> dict:
    splits = jax.random.split(jax.random.key(seed), 6)
    density_panel = normal_values(splits[0], (ROWS, INNER), 1.0, 6.0, ((0, 24), (1, 32)))
    density_pattern = plant((jax.random.randint(splits[1], (N_ROW * RB, GROUPS * KB), 0, 2) < 1).astype(jnp.int32), jax.random.fold_in(splits[1], 1), 0, 1)
    margin_blocks = normal_values(splits[2], (N_ROW, N_COL * NS, BS, BS), (SECTIONS * KB * BS) ** -0.5, 0.3125, ((0, 24), (1, 32)))
    margin_owner_keys = jax.random.split(jax.random.fold_in(splits[3], 1), N_ROW * (N_COL * NS) // NS)
    margin_owner_turns = jax.random.permutation(jax.random.fold_in(splits[3], 3), N_ROW * (N_COL * NS) // NS)
    margin_owner = jax.vmap(lambda own, number: shared_out(jax.random.fold_in(splits[3], 2), own, number, NS, N_COL, 1, CAP, 2))(margin_owner_keys, margin_owner_turns).reshape((N_ROW, N_COL * NS, 1))
    margin_place = plant(jax.random.randint(splits[4], (N_ROW, N_COL * NS), 0, N_COL * KB * CB), jax.random.fold_in(splits[4], 1), 0, (N_COL * KB * CB) - 1).astype(jnp.int32)
    return {"density_panel": density_panel, "density_pattern": density_pattern, "margin_blocks": margin_blocks, "margin_owner": margin_owner, "margin_place": margin_place}


def settle(item):
    blocks, labels = item
    flat = blocks.astype(jnp.float32).reshape(N_COL * NS, BS * BS)
    summed = jax.ops.segment_sum(flat, labels, num_segments=N_COL * N_COL * KB * CB)
    return summed.astype(jnp.bfloat16)


def multiply(item):
    left, right = item
    return jnp.einsum("cimk,cmkj->cij", left.astype(jnp.float32), right.astype(jnp.float32))


def reference(density_panel, density_pattern, margin_blocks, margin_owner, margin_place):
    common = math.gcd(N_ROW, N_COL)
    period = N_ROW * N_COL // common
    gates = density_pattern.astype(jnp.bfloat16)[:, None, :, None]
    masked = density_panel.reshape(N_ROW * RB, BS, GROUPS * KB, BS) * gates
    masked = masked.reshape(N_ROW, RB * BS, N_COL, common, N_ROW // common, KB * BS)
    labels = (margin_owner[:, :, 0] * (N_COL * KB * CB) + margin_place).astype(jnp.int32)
    dense = lax.map(settle, (margin_blocks, labels))
    dense = dense.reshape(N_ROW, N_COL, N_COL * KB, CB, BS, BS).transpose(0, 2, 4, 1, 3, 5)
    dense = dense.reshape(N_ROW, common, N_COL // common, KB * BS, N_COL, CB * BS)
    grid_rows = np.arange(N_ROW)[:, None] + np.zeros((1, N_COL), np.int64)
    grid_cols = np.arange(N_COL)[None, :] + np.zeros((N_ROW, 1), np.int64)
    total = jnp.zeros((N_ROW, N_COL, RB * BS, CB * BS), jnp.float32)
    for section in range(SECTIONS):
        turn = grid_rows + grid_cols + section
        base = turn % period
        first_left = (base - turn % N_COL) // N_COL
        first_right = (base - turn % N_ROW) // N_ROW
        left = masked[grid_rows, :, (grid_cols + section) % N_COL, :, first_left, :]
        right = dense[(grid_rows + section) % N_ROW, :, first_right, :, grid_cols, :]
        total = total + lax.map(multiply, (left, right))
    return total.transpose(0, 2, 1, 3).reshape(N_ROW * RB * BS, N_COL * CB * BS)
```

```python
import jax
import jax.numpy as jnp
from jax import lax
from jax.sharding import PartitionSpec as P

CB = 2
CAP = 2
SECTIONS = 3
WIDTH = 128


def shifted(value, axis, steps):
    count = lax.axis_size(axis)
    pairs = [(source, (source + steps) % count) for source in range(count)]
    return lax.ppermute(value, axis, pairs)


def on_device(density_panel, density_pattern, margin_blocks, margin_owner, margin_place):
    rows_here, inner_here = density_panel.shape
    row_blocks, inner_blocks = density_pattern.shape
    stack = margin_blocks.shape[1]
    row_count = lax.axis_size("row")
    col_count = lax.axis_size("col")
    row_index = lax.axis_index("row")
    col_index = lax.axis_index("col")
    common = 8
    left_turns = row_count // common
    right_turns = col_count // common
    period = row_count * right_turns

    owners = margin_owner[0, :, 0]
    places = margin_place[0]
    blocks = margin_blocks[0]
    same_owner = owners[:, None] == owners[None, :]
    earlier = jnp.arange(stack)[:, None] < jnp.arange(stack)[None, :]
    ranking = jnp.sum((same_owner & earlier).astype(jnp.int32), axis=0)
    select = (owners[None, None, :] == jnp.arange(col_count)[:, None, None]) & (
        ranking[None, None, :] == jnp.arange(CAP)[None, :, None]
    )
    outgoing = jnp.einsum(
        "dkn,nxy->dkxy", select.astype(jnp.bfloat16), blocks, preferred_element_type=jnp.float32
    ).astype(jnp.bfloat16)
    targets = jnp.sum(select.astype(jnp.int32) * (places + 1)[None, None, :], axis=2) - 1
    incoming = lax.all_to_all(outgoing, "col", split_axis=0, concat_axis=0, tiled=True)
    landing = lax.all_to_all(targets, "col", split_axis=0, concat_axis=0, tiled=True)

    left_view = density_panel.reshape(rows_here, common, left_turns, WIDTH)
    gate_view = density_pattern.reshape(row_blocks, common, left_turns)

    def left_part(section):
        home = lax.rem(col_index + col_count - section, col_count)
        turn = lax.rem(row_index + home + section, period)
        first = turn // col_count
        part = lax.dynamic_index_in_dim(left_view, first, 2, keepdims=False)
        gate = lax.dynamic_index_in_dim(gate_view, first, 2, keepdims=False).astype(jnp.bfloat16)
        part = part.reshape(row_blocks, WIDTH, common, WIDTH) * gate[:, None, :, None]
        return part.reshape(rows_here, common * WIDTH)

    lefts = [left_part(0)] + [shifted(left_part(s), "col", -s) for s in range(1, SECTIONS)]

    slot_count = col_count * CAP
    landing = landing.reshape(slot_count)
    wanted = []
    for section in range(SECTIONS):
        home = lax.rem(row_index + row_count - section, row_count)
        turn = lax.rem(home + col_index + section, period)
        first = turn // row_count
        inner = first + right_turns * jnp.arange(common)
        wanted.append((inner[:, None] * CB + jnp.arange(CB)[None, :]).reshape(-1))
    wanted = jnp.stack(wanted)
    onehot = (landing[None, None, :] == wanted[:, :, None]).astype(jnp.bfloat16)
    dense = jnp.einsum(
        "aps,sxy->apxy",
        onehot,
        incoming.reshape(slot_count, WIDTH, WIDTH),
        preferred_element_type=jnp.float32,
    ).astype(jnp.bfloat16)
    dense = dense.reshape(SECTIONS, common, CB, WIDTH, WIDTH).transpose(0, 1, 3, 2, 4)
    dense = dense.reshape(SECTIONS, common * WIDTH, CB * WIDTH)
    rights = [dense[0]] + [shifted(dense[s], "row", -s) for s in range(1, SECTIONS)]
    total = jnp.dot(lefts[0], rights[0], preferred_element_type=jnp.float32)
    for section in range(1, SECTIONS):
        total = total + jnp.dot(lefts[section], rights[section], preferred_element_type=jnp.float32)
    return total


def solution(mesh):
    return jax.shard_map(
        on_device,
        mesh=mesh,
        in_specs=(
            P("row", "col"),
            P("row", "col"),
            P("row", "col", None, None),
            P("row", "col", None),
            P("row", "col"),
        ),
        out_specs=P("row", "col"),
        check_vma=False,
    )
```

```python
import jax
import jax.numpy as jnp
from jax import lax
from jax.experimental import pallas as pl
from jax.experimental.pallas import tpu as pltpu
from jax.sharding import PartitionSpec as P

MESH = pl.DeviceIdType.MESH
NR = 24
NC = 32
W = 128
M = 8
LT = 3
RT = 4
ROWS = 512
CHUNKS = 4
DEEP = M * W // CHUNKS


def spread(c):
    return c // 8, (c // 2) % 4, c % 2


def joined(x, y, k):
    return lax.rem(x + 4, 4) * 8 + lax.rem(y + 4, 4) * 2 + lax.rem(k + 2, 2)


def kernel(
    meta, pattern, density, blocks, out,
    blk, a_own, a_ext, a_r1, a_r2, send, recv, relay, msend, mrecv, mrelay,
    acc, acc_x, b_own, b_ext, b_r1, b_r2,
    in_sem, d_send, d_recv, m_send, m_recv, y_send, y_recv, n_send, n_recv,
    a2_send, a2_recv, a1_send, a1_recv, b2_send, b2_recv, b1_send, b1_recv,
):
    r = lax.axis_index("row")
    c = lax.axis_index("col")
    x, y, k = spread(c)

    def at_offset(d, sign):
        dx, dy, dk = spread(d)
        return joined(x + sign * dx, y + sign * dy, k + dk)

    barrier = pltpu.get_barrier_semaphore()

    def greet(d, carry):
        pl.semaphore_signal(
            barrier, inc=1, device_id=(r, lax.rem(c + d, NC)), device_id_type=MESH
        )
        return carry

    lax.fori_loop(1, NC, greet, 0)
    near = r + 1 - 2 * lax.rem(r, 2)
    above = lax.rem(r + 2, NR)
    below = lax.rem(r + NR - 2, NR)
    pl.semaphore_signal(barrier, inc=1, device_id=(near, c), device_id_type=MESH)
    pl.semaphore_signal(barrier, inc=1, device_id=(above, c), device_id_type=MESH)

    own_first = (r + c) // NC
    ext_first = (r + lax.rem(c + NC - 2, NC) + 2) // NC

    def block_load():
        return pltpu.make_async_copy(blocks, blk, in_sem.at[0])

    def panel_load(first, place, sem, m):
        return pltpu.make_async_copy(
            density.at[:, pl.ds(pl.multiple_of((first + LT * m) * W, W), W)],
            place.at[:, m * W:(m + 1) * W],
            in_sem.at[sem + m],
        )

    block_load().start()
    for m in range(M):
        panel_load(ext_first, a_ext, 1, m).start()
    for m in range(M):
        panel_load(own_first, a_own, 1 + M, m).start()

    block_load().wait()

    def pack(d, carry):
        owner = at_offset(d, 1)
        low = meta[0, owner]
        high = meta[1, owner]
        send[d, 0] = blk[jnp.maximum(low, 0) // 64]
        send[d, 1] = blk[jnp.maximum(high, 0) // 64]
        low = jnp.where(low < 0, -1, lax.rem(jnp.maximum(low, 0), 64))
        high = jnp.where(high < 0, -1, lax.rem(jnp.maximum(high, 0), 64))
        msend[d, 0:1] = jnp.full((1, W), low, jnp.int32)
        msend[d, 1:2] = jnp.full((1, W), high, jnp.int32)
        return carry

    lax.fori_loop(0, NC, pack, 0)

    def gate(first, place):
        def one(i, carry):
            rows = pl.ds(pl.multiple_of(i * W, W), W)
            for m in range(M):
                keep = pattern[i, first + LT * m] != 0
                value = place[rows, m * W:(m + 1) * W]
                place[rows, m * W:(m + 1) * W] = jnp.where(keep, value, jnp.zeros_like(value))
            return carry

        lax.fori_loop(0, ROWS // W, one, 0)

    for m in range(M):
        panel_load(ext_first, a_ext, 1, m).wait()
    gate(ext_first, a_ext)

    pl.semaphore_wait(barrier, NC + 1)

    def direct(d):
        to = (r, at_offset(d, 1))
        return (
            pltpu.make_async_remote_copy(
                send.at[d], recv.at[d], d_send.at[d], d_recv.at[d], device_id=to, device_id_type=MESH
            ),
            pltpu.make_async_remote_copy(
                msend.at[d], mrecv.at[d], m_send.at[d], m_recv.at[d], device_id=to, device_id_type=MESH
            ),
        )

    def offset_of(e, dy):
        return (e // 2) * 8 + dy * 2 + lax.rem(e, 2)

    def first_leg(e):
        d = offset_of(e, 2)
        to = (r, at_offset(offset_of(e, 1), 1))
        return (
            pltpu.make_async_remote_copy(
                send.at[d], relay.at[e], d_send.at[d], y_recv.at[e], device_id=to, device_id_type=MESH
            ),
            pltpu.make_async_remote_copy(
                msend.at[d], mrelay.at[e], m_send.at[d], n_recv.at[e], device_id=to, device_id_type=MESH
            ),
        )

    def second_leg(e):
        d = offset_of(e, 2)
        to = (r, joined(x, y + 1, k))
        return (
            pltpu.make_async_remote_copy(
                relay.at[e], recv.at[d], y_send.at[e], d_recv.at[d], device_id=to, device_id_type=MESH
            ),
            pltpu.make_async_remote_copy(
                mrelay.at[e], mrecv.at[d], n_send.at[e], m_recv.at[d], device_id=to, device_id_type=MESH
            ),
        )

    def panel_shift(i):
        rows = pl.ds(pl.multiple_of(i * W, W), W)
        return pltpu.make_async_remote_copy(
            a_ext.at[rows], a_r2.at[rows], a2_send.at[i], a2_recv.at[i],
            device_id=(r, lax.rem(c + NC - 2, NC)), device_id_type=MESH,
        )

    def panel_across(source, i):
        rows = pl.ds(pl.multiple_of(i * W, W), W)
        return pltpu.make_async_remote_copy(
            source.at[rows], a_r1.at[rows], a1_send.at[i], a1_recv.at[i],
            device_id=(r, c + 1 - 2 * k), device_id_type=MESH,
        )

    def go(pair):
        for one in pair:
            one.start()

    def send_out(e, carry):
        go(first_leg(e))
        go(direct(offset_of(e, 3)))
        go(direct(offset_of(e, 1)))

        @pl.when(e % 2 == 1)
        def _():
            panel_shift(e // 2).start()

        @pl.when(e > 0)
        def _():
            go(direct(offset_of(e, 0)))

        return carry

    lax.fori_loop(0, 8, send_out, 0)

    recv[0] = send[0]
    mrecv[0] = msend[0]
    for m in range(M):
        panel_load(own_first, a_own, 1 + M, m).wait()
    gate(own_first, a_own)

    @pl.when(k == 1)
    def _():
        def one(i, carry):
            panel_across(a_own, i).start()
            return carry

        lax.fori_loop(0, CHUNKS, one, 0)

    def pass_on(e, carry):
        for one in first_leg(e):
            one.wait_recv()
        go(second_leg(e))
        return carry

    lax.fori_loop(0, 8, pass_on, 0)

    right_first = (r + c) // NR

    def gathered(position, first, dy):
        wanted = 2 * first + 8 * (position // 2) + lax.rem(position, 2)
        total = jnp.zeros((W, W), jnp.float32)
        for e in range(8):
            d = (e // 2) * 8 + dy * 2 + e % 2
            for s in range(2):
                hit = jnp.broadcast_to(mrecv[d, s:s + 1], (W, W)) == wanted
                total = total + jnp.where(hit, recv[d, s].astype(jnp.float32), 0.0)
        return total

    def where_at(m):
        return pl.ds(pl.multiple_of(m * W, W), W)

    def add_group(dy, fresh):
        def one(m, carry):
            for q in range(2):
                lanes = slice(q * W, (q + 1) * W)
                value = gathered(2 * m + q, right_first, dy)
                acc[where_at(m), lanes] = value if fresh else acc[where_at(m), lanes] + value

                @pl.when(r < 2)
                def _():
                    value = gathered(2 * m + q, right_first + 1, dy)
                    acc_x[where_at(m), lanes] = value if fresh else acc_x[where_at(m), lanes] + value

            return carry

        lax.fori_loop(0, M, one, 0)

    def arrived(dy):
        def one(e, carry):
            d = offset_of(e, dy)

            @pl.when(d > 0)
            def _():
                for copy in direct(d):
                    copy.wait_recv()

            return carry

        lax.fori_loop(0, 8, one, 0)

    arrived(0)
    add_group(0, True)
    arrived(3)
    add_group(3, False)
    arrived(1)
    add_group(1, False)
    arrived(2)

    def down_two(ch):
        rows = pl.ds(pl.multiple_of(ch * DEEP, DEEP), DEEP)
        return pltpu.make_async_remote_copy(
            b_ext.at[rows], b_r2.at[rows], b2_send.at[ch], b2_recv.at[ch],
            device_id=(below, c), device_id_type=MESH,
        )

    def beside(source, ch):
        rows = pl.ds(pl.multiple_of(ch * DEEP, DEEP), DEEP)
        return pltpu.make_async_remote_copy(
            source.at[rows], b_r1.at[rows], b1_send.at[ch], b1_recv.at[ch],
            device_id=(near, c), device_id_type=MESH,
        )

    odd = lax.rem(r, 2) == 1

    def finish(ch, carry):
        for half in range(M // CHUNKS):
            m = ch * (M // CHUNKS) + half
            for q in range(2):
                lanes = slice(q * W, (q + 1) * W)
                value = (acc[where_at(m), lanes] + gathered(2 * m + q, right_first, 2)).astype(jnp.bfloat16)
                b_own[where_at(m), lanes] = value

                @pl.when(r >= 2)
                def _():
                    b_ext[where_at(m), lanes] = value

                @pl.when(r < 2)
                def _():
                    b_ext[where_at(m), lanes] = (
                        acc_x[where_at(m), lanes] + gathered(2 * m + q, right_first + 1, 2)
                    ).astype(jnp.bfloat16)

        down_two(ch).start()

        @pl.when(odd)
        def _():
            beside(b_own, ch).start()

        return carry

    lax.fori_loop(0, CHUNKS, finish, 0)

    def add_product(left, right, ch):
        depth = pl.ds(pl.multiple_of(ch * DEEP, DEEP), DEEP)
        out[...] += jnp.dot(left[:, depth], right[depth, :], preferred_element_type=jnp.float32)

    def panel_arrives(i, carry):
        panel_shift(i).wait_recv()

        @pl.when(k == 0)
        def _():
            panel_across(a_r2, i).start()

        return carry

    lax.fori_loop(0, CHUNKS, panel_arrives, 0)
    out[...] = jnp.zeros_like(out)

    def local_part(ch, carry):
        add_product(a_own, b_own, ch)
        return carry

    lax.fori_loop(0, CHUNKS, local_part, 0)

    def two_up(ch, carry):
        down_two(ch).wait_recv()

        @pl.when(jnp.logical_not(odd))
        def _():
            beside(b_r2, ch).start()

        add_product(a_r2, b_r2, ch)
        return carry

    lax.fori_loop(0, CHUNKS, two_up, 0)

    def across_arrives(i, carry):
        panel_across(a_own, i).wait_recv()
        return carry

    lax.fori_loop(0, CHUNKS, across_arrives, 0)

    def one_up(ch, carry):
        beside(b_own, ch).wait_recv()
        add_product(a_r1, b_r1, ch)
        return carry

    lax.fori_loop(0, CHUNKS, one_up, 0)

    def sent(d, carry):
        for copy in direct(d):
            copy.wait_send()
        return carry

    lax.fori_loop(1, NC, sent, 0)

    def passed(e, carry):
        for copy in second_leg(e):
            copy.wait_send()
        return carry

    lax.fori_loop(0, 8, passed, 0)

    def rest(i, carry):
        panel_shift(i).wait_send()
        panel_across(a_own, i).wait_send()
        down_two(i).wait_send()
        beside(b_own, i).wait_send()
        return carry

    lax.fori_loop(0, CHUNKS, rest, 0)


def on_device(density_panel, density_pattern, margin_blocks, margin_owner, margin_place):
    stack = margin_blocks.shape[1]
    owners = margin_owner[0, :, 0]
    code = jnp.arange(stack) * 64 + margin_place[0]
    mine = owners[None, :] == jnp.arange(NC)[:, None]
    low = jnp.min(jnp.where(mine, code[None, :], stack * 64), axis=1)
    high = jnp.max(jnp.where(mine, code[None, :], -1), axis=1)
    meta = jnp.stack([jnp.where(high < 0, -1, low), jnp.where(high == low, -1, high)])
    bf16, f32, i32 = jnp.bfloat16, jnp.float32, jnp.int32
    dma = pltpu.SemaphoreType.DMA
    return pl.pallas_call(
        kernel,
        out_shape=jax.ShapeDtypeStruct((ROWS, 2 * W), f32),
        in_specs=[
            pl.BlockSpec(memory_space=pltpu.SMEM),
            pl.BlockSpec(memory_space=pltpu.SMEM),
            pl.BlockSpec(memory_space=pl.ANY),
            pl.BlockSpec(memory_space=pl.ANY),
        ],
        out_specs=pl.BlockSpec(memory_space=pltpu.VMEM),
        scratch_shapes=[
            pltpu.VMEM((stack, W, W), bf16),
            pltpu.VMEM((ROWS, M * W), bf16),
            pltpu.VMEM((ROWS, M * W), bf16),
            pltpu.VMEM((ROWS, M * W), bf16),
            pltpu.VMEM((ROWS, M * W), bf16),
            pltpu.VMEM((NC, 2, W, W), bf16),
            pltpu.VMEM((NC, 2, W, W), bf16),
            pltpu.VMEM((8, 2, W, W), bf16),
            pltpu.VMEM((NC, 2, W), i32),
            pltpu.VMEM((NC, 2, W), i32),
            pltpu.VMEM((8, 2, W), i32),
            pltpu.VMEM((M * W, 2 * W), f32),
            pltpu.VMEM((M * W, 2 * W), f32),
            pltpu.VMEM((M * W, 2 * W), bf16),
            pltpu.VMEM((M * W, 2 * W), bf16),
            pltpu.VMEM((M * W, 2 * W), bf16),
            pltpu.VMEM((M * W, 2 * W), bf16),
            dma((1 + 2 * M,)),
            dma((NC,)), dma((NC,)), dma((NC,)), dma((NC,)),
            dma((8,)), dma((8,)), dma((8,)), dma((8,)),
            dma((CHUNKS,)), dma((CHUNKS,)), dma((CHUNKS,)), dma((CHUNKS,)),
            dma((CHUNKS,)), dma((CHUNKS,)), dma((CHUNKS,)), dma((CHUNKS,)),
        ],
        compiler_params=pltpu.CompilerParams(
            collective_id=0, has_side_effects=True, vmem_limit_bytes=48 * 1024 * 1024
        ),
        cost_estimate=pl.CostEstimate(flops=2 * ROWS * 3 * M * W * 2 * W, bytes_accessed=6 << 20, transcendentals=0),
    )(meta, density_pattern, density_panel, margin_blocks[0])


def solution(mesh):
    return jax.shard_map(
        on_device,
        mesh=mesh,
        in_specs=(
            P("row", "col"),
            P("row", "col"),
            P("row", "col", None, None),
            P("row", "col", None),
            P("row", "col"),
        ),
        out_specs=P("row", "col"),
        check_vma=False,
    )
```

```python
import jax
import jax.numpy as jnp
from jax import lax
from jax.experimental import pallas as pl
from jax.experimental.pallas import tpu as pltpu
from jax.sharding import PartitionSpec as P

MESH = pl.DeviceIdType.MESH
NR = 24
NC = 32
W = 128
M = 8
LT = 3
RT = 4
ROWS = 512
CHUNKS = 4
DEEP = M * W // CHUNKS


def spread(c):
    return c // 8, (c // 2) % 4, c % 2


def joined(x, y, k):
    return lax.rem(x + 4, 4) * 8 + lax.rem(y + 4, 4) * 2 + lax.rem(k + 2, 2)


def kernel(
    low, high, places, pattern, density, blocks, out,
    blk, a_own, a_ext, a_r1, a_r2, send, recv, relay, msend, mrecv, mrelay,
    acc, acc_x, b_own, b_ext, b_r1, b_r2,
    in_sem, d_send, d_recv, m_send, m_recv, y_send, y_recv, n_send, n_recv,
    a2_send, a2_recv, a1_send, a1_recv, b2_send, b2_recv, b1_send, b1_recv,
):
    r = lax.axis_index("row")
    c = lax.axis_index("col")
    x, y, k = spread(c)

    def at_offset(d, sign):
        dx, dy, dk = spread(d)
        return joined(x + sign * dx, y + sign * dy, k + dk)

    barrier = pltpu.get_barrier_semaphore()

    def greet(d, carry):
        pl.semaphore_signal(
            barrier, inc=1, device_id=(r, lax.rem(c + d, NC)), device_id_type=MESH
        )
        return carry

    lax.fori_loop(1, NC, greet, 0)
    near = r + 1 - 2 * lax.rem(r, 2)
    above = lax.rem(r + 2, NR)
    below = lax.rem(r + NR - 2, NR)
    pl.semaphore_signal(barrier, inc=1, device_id=(near, c), device_id_type=MESH)
    pl.semaphore_signal(barrier, inc=1, device_id=(above, c), device_id_type=MESH)

    own_first = (r + c) // NC
    ext_first = (r + lax.rem(c + NC - 2, NC) + 2) // NC

    def block_load():
        return pltpu.make_async_copy(blocks, blk, in_sem.at[0])

    def panel_load(first, place, sem, m):
        return pltpu.make_async_copy(
            density.at[:, pl.ds(pl.multiple_of((first + LT * m) * W, W), W)],
            place.at[:, m * W:(m + 1) * W],
            in_sem.at[sem + m],
        )

    block_load().start()
    for m in range(M):
        panel_load(ext_first, a_ext, 1, m).start()
    for m in range(M):
        panel_load(own_first, a_own, 1 + M, m).start()

    def pack(d):
        owner = at_offset(d, 1)
        one = low[owner]
        two = high[owner]
        first = jnp.where(two < 0, 0, one)
        second = jnp.maximum(two, 0)
        send[d, 0] = blk[first]
        send[d, 1] = blk[second]
        first = jnp.where(two < 0, -1, places[0, first])
        second = jnp.where((two < 0) | (two == one), -1, places[0, second])
        msend[d, 0:1] = jnp.full((1, W), first, jnp.int32)
        msend[d, 1:2] = jnp.full((1, W), second, jnp.int32)

    def gate(first, place):
        def one(i, carry):
            rows = pl.ds(pl.multiple_of(i * W, W), W)
            for m in range(M):
                keep = pattern[i, first + LT * m] != 0
                value = place[rows, m * W:(m + 1) * W]
                place[rows, m * W:(m + 1) * W] = jnp.where(keep, value, jnp.zeros_like(value))
            return carry

        lax.fori_loop(0, ROWS // W, one, 0)

    block_load().wait()
    pl.semaphore_wait(barrier, NC + 1)

    def direct(d):
        to = (r, at_offset(d, 1))
        return (
            pltpu.make_async_remote_copy(
                send.at[d], recv.at[d], d_send.at[d], d_recv.at[d], device_id=to, device_id_type=MESH
            ),
            pltpu.make_async_remote_copy(
                msend.at[d], mrecv.at[d], m_send.at[d], m_recv.at[d], device_id=to, device_id_type=MESH
            ),
        )

    def offset_of(e, dy):
        return (e // 2) * 8 + dy * 2 + lax.rem(e, 2)

    def first_leg(e):
        d = offset_of(e, 2)
        to = (r, at_offset(offset_of(e, 1), 1))
        return (
            pltpu.make_async_remote_copy(
                send.at[d], relay.at[e], d_send.at[d], y_recv.at[e], device_id=to, device_id_type=MESH
            ),
            pltpu.make_async_remote_copy(
                msend.at[d], mrelay.at[e], m_send.at[d], n_recv.at[e], device_id=to, device_id_type=MESH
            ),
        )

    def second_leg(e):
        d = offset_of(e, 2)
        to = (r, joined(x, y + 1, k))
        return (
            pltpu.make_async_remote_copy(
                relay.at[e], recv.at[d], y_send.at[e], d_recv.at[d], device_id=to, device_id_type=MESH
            ),
            pltpu.make_async_remote_copy(
                mrelay.at[e], mrecv.at[d], n_send.at[e], m_recv.at[d], device_id=to, device_id_type=MESH
            ),
        )

    def panel_shift(i):
        rows = pl.ds(pl.multiple_of(i * W, W), W)
        return pltpu.make_async_remote_copy(
            a_ext.at[rows], a_r2.at[rows], a2_send.at[i], a2_recv.at[i],
            device_id=(r, lax.rem(c + NC - 2, NC)), device_id_type=MESH,
        )

    def panel_across(source, i):
        rows = pl.ds(pl.multiple_of(i * W, W), W)
        return pltpu.make_async_remote_copy(
            source.at[rows], a_r1.at[rows], a1_send.at[i], a1_recv.at[i],
            device_id=(r, c + 1 - 2 * k), device_id_type=MESH,
        )

    def go(pair):
        for one in pair:
            one.start()

    def send_first(e, carry):
        pack(offset_of(e, 2))
        go(first_leg(e))
        pack(offset_of(e, 3))
        go(direct(offset_of(e, 3)))
        return carry

    lax.fori_loop(0, 8, send_first, 0)

    def send_next(e, carry):
        pack(offset_of(e, 1))
        go(direct(offset_of(e, 1)))

        pack(offset_of(e, 0))

        @pl.when(e > 0)
        def _():
            go(direct(offset_of(e, 0)))

        return carry

    lax.fori_loop(0, 8, send_next, 0)

    for m in range(M):
        panel_load(ext_first, a_ext, 1, m).wait()
    gate(ext_first, a_ext)

    def send_panel(i, carry):
        panel_shift(i).start()
        return carry

    lax.fori_loop(0, CHUNKS, send_panel, 0)

    recv[0] = send[0]
    mrecv[0] = msend[0]
    for m in range(M):
        panel_load(own_first, a_own, 1 + M, m).wait()
    gate(own_first, a_own)

    @pl.when(k == 1)
    def _():
        def one(i, carry):
            panel_across(a_own, i).start()
            return carry

        lax.fori_loop(0, CHUNKS, one, 0)

    def pass_on(e, carry):
        for one in first_leg(e):
            one.wait_recv()
        go(second_leg(e))
        return carry

    lax.fori_loop(0, 8, pass_on, 0)

    right_first = (r + c) // NR

    def where_at(m):
        return pl.ds(pl.multiple_of(m * W, W), W)

    def add_pair(d):
        values = [recv[d, s].astype(jnp.float32).reshape(W // 8, 8, W) for s in range(2)]
        places = [jnp.broadcast_to(mrecv[d, s:s + 1], (8, W)) for s in range(2)]

        def into(sums, first):
            def one(m, carry):
                for q in range(2):
                    total = sums[2 * m + q]
                    for s in range(2):
                        hit = (places[s] == 2 * first + 8 * m + q)[None]
                        total = total + jnp.where(hit, values[s], 0.0)
                    sums[2 * m + q] = total
                return carry

            lax.fori_loop(0, M, one, 0)

        into(acc, right_first)

        @pl.when(r < 2)
        def _():
            into(acc_x, right_first + 1)

    def take(d):
        for copy in direct(d):
            copy.wait_recv()
        add_pair(d)

    def clear(position, carry):
        acc[position] = jnp.zeros((W // 8, 8, W), jnp.float32)
        acc_x[position] = jnp.zeros((W // 8, 8, W), jnp.float32)
        return carry

    lax.fori_loop(0, 2 * M, clear, 0)
    add_pair(0)

    def take_behind(e, carry):
        take(offset_of(e, 3))
        return carry

    lax.fori_loop(0, 8, take_behind, 0)

    def take_ahead(e, carry):
        take(offset_of(e, 1))

        @pl.when(e > 0)
        def _():
            take(offset_of(e, 0))

        return carry

    lax.fori_loop(0, 8, take_ahead, 0)

    def take_far(e, carry):
        take(offset_of(e, 2))
        return carry

    lax.fori_loop(0, 8, take_far, 0)

    def down_two(ch):
        rows = pl.ds(pl.multiple_of(ch * DEEP, DEEP), DEEP)
        return pltpu.make_async_remote_copy(
            b_ext.at[rows], b_r2.at[rows], b2_send.at[ch], b2_recv.at[ch],
            device_id=(below, c), device_id_type=MESH,
        )

    def beside(source, ch):
        rows = pl.ds(pl.multiple_of(ch * DEEP, DEEP), DEEP)
        return pltpu.make_async_remote_copy(
            source.at[rows], b_r1.at[rows], b1_send.at[ch], b1_recv.at[ch],
            device_id=(near, c), device_id_type=MESH,
        )

    odd = lax.rem(r, 2) == 1

    def finish(ch, carry):
        for half in range(M // CHUNKS):
            m = ch * (M // CHUNKS) + half
            for q in range(2):
                lanes = slice(q * W, (q + 1) * W)
                value = acc[2 * m + q].reshape(W, W).astype(jnp.bfloat16)
                b_own[where_at(m), lanes] = value

                @pl.when(r >= 2)
                def _():
                    b_ext[where_at(m), lanes] = value

                @pl.when(r < 2)
                def _():
                    b_ext[where_at(m), lanes] = acc_x[2 * m + q].reshape(W, W).astype(jnp.bfloat16)

        down_two(ch).start()

        @pl.when(odd)
        def _():
            beside(b_own, ch).start()

        return carry

    lax.fori_loop(0, CHUNKS, finish, 0)

    def add_product(left, right, ch):
        depth = pl.ds(pl.multiple_of(ch * DEEP, DEEP), DEEP)
        out[...] += jnp.dot(left[:, depth], right[depth, :], preferred_element_type=jnp.float32)

    def panel_arrives(i, carry):
        panel_shift(i).wait_recv()

        @pl.when(k == 0)
        def _():
            panel_across(a_r2, i).start()

        return carry

    lax.fori_loop(0, CHUNKS, panel_arrives, 0)
    out[...] = jnp.zeros_like(out)

    def local_part(ch, carry):
        add_product(a_own, b_own, ch)
        return carry

    lax.fori_loop(0, CHUNKS, local_part, 0)

    def two_up(ch, carry):
        down_two(ch).wait_recv()

        @pl.when(jnp.logical_not(odd))
        def _():
            beside(b_r2, ch).start()

        add_product(a_r2, b_r2, ch)
        return carry

    lax.fori_loop(0, CHUNKS, two_up, 0)

    def across_arrives(i, carry):
        panel_across(a_own, i).wait_recv()
        return carry

    lax.fori_loop(0, CHUNKS, across_arrives, 0)

    def one_up(ch, carry):
        beside(b_own, ch).wait_recv()
        add_product(a_r1, b_r1, ch)
        return carry

    lax.fori_loop(0, CHUNKS, one_up, 0)

    def sent(d, carry):
        for copy in direct(d):
            copy.wait_send()
        return carry

    lax.fori_loop(1, NC, sent, 0)

    def passed(e, carry):
        for copy in second_leg(e):
            copy.wait_send()
        return carry

    lax.fori_loop(0, 8, passed, 0)

    def rest(i, carry):
        panel_shift(i).wait_send()
        panel_across(a_own, i).wait_send()
        down_two(i).wait_send()
        beside(b_own, i).wait_send()
        return carry

    lax.fori_loop(0, CHUNKS, rest, 0)


def on_device(density_panel, density_pattern, margin_blocks, margin_owner, margin_place):
    stack = margin_blocks.shape[1]
    owners = margin_owner[0, :, 0]
    index = jnp.arange(stack)[None, :]
    mine = owners[None, :] == jnp.arange(NC)[:, None]
    high = jnp.max(jnp.where(mine, index, -1), axis=1)
    low = jnp.min(jnp.where(mine, index, stack), axis=1)
    bf16, f32, i32 = jnp.bfloat16, jnp.float32, jnp.int32
    dma = pltpu.SemaphoreType.DMA
    return pl.pallas_call(
        kernel,
        out_shape=jax.ShapeDtypeStruct((ROWS, 2 * W), f32),
        in_specs=[
            pl.BlockSpec(memory_space=pltpu.SMEM),
            pl.BlockSpec(memory_space=pltpu.SMEM),
            pl.BlockSpec(memory_space=pltpu.SMEM),
            pl.BlockSpec(memory_space=pltpu.SMEM),
            pl.BlockSpec(memory_space=pl.ANY),
            pl.BlockSpec(memory_space=pl.ANY),
        ],
        out_specs=pl.BlockSpec(memory_space=pltpu.VMEM),
        scratch_shapes=[
            pltpu.VMEM((stack, W, W), bf16),
            pltpu.VMEM((ROWS, M * W), bf16),
            pltpu.VMEM((ROWS, M * W), bf16),
            pltpu.VMEM((ROWS, M * W), bf16),
            pltpu.VMEM((ROWS, M * W), bf16),
            pltpu.VMEM((NC, 2, W, W), bf16),
            pltpu.VMEM((NC, 2, W, W), bf16),
            pltpu.VMEM((8, 2, W, W), bf16),
            pltpu.VMEM((NC, 2, W), i32),
            pltpu.VMEM((NC, 2, W), i32),
            pltpu.VMEM((8, 2, W), i32),
            pltpu.VMEM((2 * M, W // 8, 8, W), f32),
            pltpu.VMEM((2 * M, W // 8, 8, W), f32),
            pltpu.VMEM((M * W, 2 * W), bf16),
            pltpu.VMEM((M * W, 2 * W), bf16),
            pltpu.VMEM((M * W, 2 * W), bf16),
            pltpu.VMEM((M * W, 2 * W), bf16),
            dma((1 + 2 * M,)),
            dma((NC,)), dma((NC,)), dma((NC,)), dma((NC,)),
            dma((8,)), dma((8,)), dma((8,)), dma((8,)),
            dma((CHUNKS,)), dma((CHUNKS,)), dma((CHUNKS,)), dma((CHUNKS,)),
            dma((CHUNKS,)), dma((CHUNKS,)), dma((CHUNKS,)), dma((CHUNKS,)),
        ],
        compiler_params=pltpu.CompilerParams(
            collective_id=0, has_side_effects=True, vmem_limit_bytes=62 * 1024 * 1024
        ),
        cost_estimate=pl.CostEstimate(flops=2 * ROWS * 3 * M * W * 2 * W, bytes_accessed=6 << 20, transcendentals=0),
    )(low, high, margin_place, density_pattern, density_panel, margin_blocks[0])


def solution(mesh):
    return jax.shard_map(
        on_device,
        mesh=mesh,
        in_specs=(
            P("row", "col"),
            P("row", "col"),
            P("row", "col", None, None),
            P("row", "col", None),
            P("row", "col"),
        ),
        out_specs=P("row", "col"),
        check_vma=False,
    )
```

```python
import functools

import jax
import jax.numpy as jnp
from jax import lax
from jax.experimental import pallas as pl
from jax.experimental.pallas import tpu as pltpu
from jax.sharding import PartitionSpec as P

MESH = pl.DeviceIdType.MESH
NR = 24
NC = 32
W = 128
M = 8
LT = 3
RT = 4
ROWS = 512
CHUNKS = 4
DEEP = M * W // CHUNKS
H = W // 2


def spread(c):
    return c // 8, (c // 2) % 4, c % 2


def joined(x, y, k):
    return lax.rem(x + 4, 4) * 8 + lax.rem(y + 4, 4) * 2 + lax.rem(k + 2, 2)


def kernel(
    low, high, places, pattern, density, blocks, out,
    blk, a_own, a_ext, a_r1, a_r2, send, recv, relay, msend, mrecv, mrelay,
    acc, acc_x, b_own, b_ext, b_r1, b_r2,
    in_sem, d_send, d_recv, m_send, m_recv, y_send, y_recv, n_send, n_recv,
    a2_send, a2_recv, a1_send, a1_recv, b2_send, b2_recv, b1_send, b1_recv,
):
    r = lax.axis_index("row")
    c = lax.axis_index("col")
    x, y, k = spread(c)

    def at_offset(d, sign):
        dx, dy, dk = spread(d)
        return joined(x + sign * dx, y + sign * dy, k + dk)

    barrier = pltpu.get_barrier_semaphore()

    def greet(d, carry):
        pl.semaphore_signal(
            barrier, inc=1, device_id=(r, lax.rem(c + d, NC)), device_id_type=MESH
        )
        return carry

    lax.fori_loop(1, NC, greet, 0)
    near = r + 1 - 2 * lax.rem(r, 2)
    above = lax.rem(r + 2, NR)
    below = lax.rem(r + NR - 2, NR)
    pl.semaphore_signal(barrier, inc=1, device_id=(near, c), device_id_type=MESH)
    pl.semaphore_signal(barrier, inc=1, device_id=(above, c), device_id_type=MESH)

    own_first = (r + c) // NC
    ext_first = (r + lax.rem(c + NC - 2, NC) + 2) // NC

    def block_load():
        return pltpu.make_async_copy(blocks, blk, in_sem.at[0])

    def panel_load(first, place, sem, m):
        return pltpu.make_async_copy(
            density.at[:, pl.ds(pl.multiple_of((first + LT * m) * W, W), W)],
            place.at[:, m * W:(m + 1) * W],
            in_sem.at[sem + m],
        )

    block_load().start()
    for m in range(M):
        panel_load(ext_first, a_ext, 1, m).start()
    for m in range(M):
        panel_load(own_first, a_own, 1 + M, m).start()

    def pack(d):
        owner = at_offset(d, 1)
        one = low[owner]
        two = high[owner]
        first = jnp.where(two < 0, 0, one)
        second = jnp.maximum(two, 0)
        for slot, value in ((0, blk[first]), (1, blk[second])):
            send[d, 0, slot] = value[:H]
            send[d, 1, slot] = value[H:]
        first = jnp.where(two < 0, -1, places[0, first])
        second = jnp.where((two < 0) | (two == one), -1, places[0, second])
        msend[d, 0:1] = jnp.full((1, W), first, jnp.int32)
        msend[d, 1:2] = jnp.full((1, W), second, jnp.int32)

    def gate(first, place):
        def one(i, carry):
            rows = pl.ds(pl.multiple_of(i * W, W), W)
            for m in range(M):
                keep = pattern[i, first + LT * m] != 0
                value = place[rows, m * W:(m + 1) * W]
                place[rows, m * W:(m + 1) * W] = jnp.where(keep, value, jnp.zeros_like(value))
            return carry

        lax.fori_loop(0, ROWS // W, one, 0)

    block_load().wait()
    pl.semaphore_wait(barrier, NC + 1)

    def direct(d, h):
        return pltpu.make_async_remote_copy(
            send.at[d, h], recv.at[d, h], d_send.at[d, h], d_recv.at[d, h],
            device_id=(r, at_offset(d, 1)), device_id_type=MESH,
        )

    def direct_place(d):
        return pltpu.make_async_remote_copy(
            msend.at[d], mrecv.at[d], m_send.at[d], m_recv.at[d],
            device_id=(r, at_offset(d, 1)), device_id_type=MESH,
        )

    def offset_of(e, dy):
        return (e // 2) * 8 + dy * 2 + lax.rem(e, 2)

    def first_leg(e, h):
        d = offset_of(e, 2)
        return pltpu.make_async_remote_copy(
            send.at[d, h], relay.at[e, h], d_send.at[d, h], y_recv.at[e, h],
            device_id=(r, at_offset(offset_of(e, 1), 1)), device_id_type=MESH,
        )

    def first_place(e):
        d = offset_of(e, 2)
        return pltpu.make_async_remote_copy(
            msend.at[d], mrelay.at[e], m_send.at[d], n_recv.at[e],
            device_id=(r, at_offset(offset_of(e, 1), 1)), device_id_type=MESH,
        )

    def second_leg(e, h):
        d = offset_of(e, 2)
        return pltpu.make_async_remote_copy(
            relay.at[e, h], recv.at[d, h], y_send.at[e, h], d_recv.at[d, h],
            device_id=(r, joined(x, y + 1, k)), device_id_type=MESH,
        )

    def second_place(e):
        d = offset_of(e, 2)
        return pltpu.make_async_remote_copy(
            mrelay.at[e], mrecv.at[d], n_send.at[e], m_recv.at[d],
            device_id=(r, joined(x, y + 1, k)), device_id_type=MESH,
        )

    def panel_shift(i):
        rows = pl.ds(pl.multiple_of(i * W, W), W)
        return pltpu.make_async_remote_copy(
            a_ext.at[rows], a_r2.at[rows], a2_send.at[i], a2_recv.at[i],
            device_id=(r, lax.rem(c + NC - 2, NC)), device_id_type=MESH,
        )

    def panel_across(source, i):
        rows = pl.ds(pl.multiple_of(i * W, W), W)
        return pltpu.make_async_remote_copy(
            source.at[rows], a_r1.at[rows], a1_send.at[i], a1_recv.at[i],
            device_id=(r, c + 1 - 2 * k), device_id_type=MESH,
        )

    def send_first(e, carry):
        pack(offset_of(e, 2))
        first_place(e).start()
        first_leg(e, 0).start()
        pack(offset_of(e, 3))
        direct_place(offset_of(e, 3)).start()
        direct(offset_of(e, 3), 0).start()
        return carry

    lax.fori_loop(0, 8, send_first, 0)

    def send_next(e, carry):
        pack(offset_of(e, 1))
        direct_place(offset_of(e, 1)).start()
        direct(offset_of(e, 1), 0).start()
        pack(offset_of(e, 0))

        @pl.when(e > 0)
        def _():
            direct_place(offset_of(e, 0)).start()
            direct(offset_of(e, 0), 0).start()

        return carry

    lax.fori_loop(0, 8, send_next, 0)

    def send_second(e, carry):
        first_leg(e, 1).start()
        direct(offset_of(e, 3), 1).start()
        direct(offset_of(e, 1), 1).start()

        @pl.when(e > 0)
        def _():
            direct(offset_of(e, 0), 1).start()

        return carry

    lax.fori_loop(0, 8, send_second, 0)

    for m in range(M):
        panel_load(ext_first, a_ext, 1, m).wait()
    gate(ext_first, a_ext)

    recv[0] = send[0]
    mrecv[0] = msend[0]
    for m in range(M):
        panel_load(own_first, a_own, 1 + M, m).wait()
    gate(own_first, a_own)

    @pl.when(k == 1)
    def _():
        def one(i, carry):
            panel_across(a_own, i).start()
            return carry

        lax.fori_loop(0, CHUNKS, one, 0)

    def pass_on(e, carry):
        first_place(e).wait_recv()
        first_leg(e, 0).wait_recv()
        second_place(e).start()
        second_leg(e, 0).start()

        @pl.when(e % 2 == 1)
        def _():
            panel_shift(e // 2).start()

        return carry

    lax.fori_loop(0, 8, pass_on, 0)

    right_first = (r + c) // NR

    G = H // 8

    def add_pair(d, h):
        values = [recv[d, h, slot].astype(jnp.float32).reshape(G, 8, W) for slot in range(2)]
        places = [jnp.broadcast_to(mrecv[d, slot:slot + 1], (8, W)) for slot in range(2)]

        def into(sums, first):
            def one(m, carry):
                for q in range(2):
                    total = sums[2 * m + q, h * G:(h + 1) * G]
                    for slot in range(2):
                        hit = (places[slot] == 2 * first + 8 * m + q)[None]
                        total = total + jnp.where(hit, values[slot], 0.0)
                    sums[2 * m + q, h * G:(h + 1) * G] = total
                return carry

            lax.fori_loop(0, M, one, 0)

        into(acc, right_first)

        @pl.when(r < 2)
        def _():
            into(acc_x, right_first + 1)

    def take(d, h):
        if h == 0:
            direct_place(d).wait_recv()
        direct(d, h).wait_recv()
        add_pair(d, h)

    def clear(position, carry):
        acc[position] = jnp.zeros((W // 8, 8, W), jnp.float32)
        acc_x[position] = jnp.zeros((W // 8, 8, W), jnp.float32)
        return carry

    lax.fori_loop(0, 2 * M, clear, 0)
    odd = lax.rem(r, 2) == 1

    def down_two(ch, h):
        part = pl.ds(2 * ch, 2)
        return pltpu.make_async_remote_copy(
            b_ext.at[part, h], b_r2.at[part, h], b2_send.at[ch, h], b2_recv.at[ch, h],
            device_id=(below, c), device_id_type=MESH,
        )

    def beside(source, ch, h):
        part = pl.ds(2 * ch, 2)
        return pltpu.make_async_remote_copy(
            source.at[part, h], b_r1.at[part, h], b1_send.at[ch, h], b1_recv.at[ch, h],
            device_id=(near, c), device_id_type=MESH,
        )

    def finish(h):
        def one(ch, carry):
            for half in range(2):
                m = 2 * ch + half
                for q in range(2):
                    lanes = slice(q * W, (q + 1) * W)
                    value = acc[2 * m + q, h * G:(h + 1) * G].reshape(H, W).astype(jnp.bfloat16)
                    b_own[m, h, :, lanes] = value

                    @pl.when(r >= 2)
                    def _():
                        b_ext[m, h, :, lanes] = value

                    @pl.when(r < 2)
                    def _():
                        b_ext[m, h, :, lanes] = (
                            acc_x[2 * m + q, h * G:(h + 1) * G].reshape(H, W).astype(jnp.bfloat16)
                        )

            down_two(ch, h).start()

            @pl.when(odd)
            def _():
                beside(b_own, ch, h).start()

            return carry

        lax.fori_loop(0, CHUNKS, one, 0)

    def hand_on(ch, h):
        down_two(ch, h).wait_recv()

        @pl.when(jnp.logical_not(odd))
        def _():
            beside(b_r2, ch, h).start()

    def take_behind(e, carry, h):
        take(offset_of(e, 3), h)
        return carry

    def take_ahead(e, carry, h):
        if h == 0:
            first_leg(e, 1).wait_recv()
            second_leg(e, 1).start()
        take(offset_of(e, 1), h)

        @pl.when(e > 0)
        def _():
            take(offset_of(e, 0), h)

        return carry

    def take_far(e, carry, h):
        take(offset_of(e, 2), h)
        if h == 1:

            @pl.when(e % 2 == 1)
            def _():
                hand_on(e // 2, 0)

        return carry

    for h in range(2):
        add_pair(0, h)
        lax.fori_loop(0, 8, functools.partial(take_behind, h=h), 0)
        lax.fori_loop(0, 8, functools.partial(take_ahead, h=h), 0)
        lax.fori_loop(0, 8, functools.partial(take_far, h=h), 0)
        finish(h)

    def add_product(left, right, ch):
        depth = pl.ds(pl.multiple_of(ch * DEEP, DEEP), DEEP)
        piece = right[pl.ds(2 * ch, 2)].reshape(DEEP, 2 * W)
        out[...] += jnp.dot(left[:, depth], piece, preferred_element_type=jnp.float32)

    def panel_arrives(i, carry):
        panel_shift(i).wait_recv()

        @pl.when(k == 0)
        def _():
            panel_across(a_r2, i).start()

        return carry

    lax.fori_loop(0, CHUNKS, panel_arrives, 0)
    out[...] = jnp.zeros_like(out)

    def local_part(ch, carry):
        add_product(a_own, b_own, ch)
        return carry

    lax.fori_loop(0, CHUNKS, local_part, 0)

    def two_up(ch, carry):
        hand_on(ch, 1)
        add_product(a_r2, b_r2, ch)
        return carry

    lax.fori_loop(0, CHUNKS, two_up, 0)

    def across_arrives(i, carry):
        panel_across(a_own, i).wait_recv()
        return carry

    lax.fori_loop(0, CHUNKS, across_arrives, 0)

    def one_up(ch, carry):
        beside(b_own, ch, 0).wait_recv()
        beside(b_own, ch, 1).wait_recv()
        add_product(a_r1, b_r1, ch)
        return carry

    lax.fori_loop(0, CHUNKS, one_up, 0)

    def sent(d, carry):
        direct_place(d).wait_send()
        direct(d, 0).wait_send()
        direct(d, 1).wait_send()
        return carry

    lax.fori_loop(1, NC, sent, 0)

    def passed(e, carry):
        second_place(e).wait_send()
        second_leg(e, 0).wait_send()
        second_leg(e, 1).wait_send()
        return carry

    lax.fori_loop(0, 8, passed, 0)

    def rest(i, carry):
        panel_shift(i).wait_send()
        panel_across(a_own, i).wait_send()
        for h in range(2):
            down_two(i, h).wait_send()
            beside(b_own, i, h).wait_send()
        return carry

    lax.fori_loop(0, CHUNKS, rest, 0)


def on_device(density_panel, density_pattern, margin_blocks, margin_owner, margin_place):
    stack = margin_blocks.shape[1]
    owners = margin_owner[0, :, 0]
    index = jnp.arange(stack)[None, :]
    mine = owners[None, :] == jnp.arange(NC)[:, None]
    high = jnp.max(jnp.where(mine, index, -1), axis=1)
    low = jnp.min(jnp.where(mine, index, stack), axis=1)
    bf16, f32, i32 = jnp.bfloat16, jnp.float32, jnp.int32
    dma = pltpu.SemaphoreType.DMA
    return pl.pallas_call(
        kernel,
        out_shape=jax.ShapeDtypeStruct((ROWS, 2 * W), f32),
        in_specs=[
            pl.BlockSpec(memory_space=pltpu.SMEM),
            pl.BlockSpec(memory_space=pltpu.SMEM),
            pl.BlockSpec(memory_space=pltpu.SMEM),
            pl.BlockSpec(memory_space=pltpu.SMEM),
            pl.BlockSpec(memory_space=pl.ANY),
            pl.BlockSpec(memory_space=pl.ANY),
        ],
        out_specs=pl.BlockSpec(memory_space=pltpu.VMEM),
        scratch_shapes=[
            pltpu.VMEM((stack, W, W), bf16),
            pltpu.VMEM((ROWS, M * W), bf16),
            pltpu.VMEM((ROWS, M * W), bf16),
            pltpu.VMEM((ROWS, M * W), bf16),
            pltpu.VMEM((ROWS, M * W), bf16),
            pltpu.VMEM((NC, 2, 2, H, W), bf16),
            pltpu.VMEM((NC, 2, 2, H, W), bf16),
            pltpu.VMEM((8, 2, 2, H, W), bf16),
            pltpu.VMEM((NC, 2, W), i32),
            pltpu.VMEM((NC, 2, W), i32),
            pltpu.VMEM((8, 2, W), i32),
            pltpu.VMEM((2 * M, W // 8, 8, W), f32),
            pltpu.VMEM((2 * M, W // 8, 8, W), f32),
            pltpu.VMEM((M, 2, H, 2 * W), bf16),
            pltpu.VMEM((M, 2, H, 2 * W), bf16),
            pltpu.VMEM((M, 2, H, 2 * W), bf16),
            pltpu.VMEM((M, 2, H, 2 * W), bf16),
            dma((1 + 2 * M,)),
            dma((NC, 2)), dma((NC, 2)), dma((NC,)), dma((NC,)),
            dma((8, 2)), dma((8, 2)), dma((8,)), dma((8,)),
            dma((CHUNKS,)), dma((CHUNKS,)), dma((CHUNKS,)), dma((CHUNKS,)),
            dma((CHUNKS, 2)), dma((CHUNKS, 2)), dma((CHUNKS, 2)), dma((CHUNKS, 2)),
        ],
        compiler_params=pltpu.CompilerParams(
            collective_id=0, has_side_effects=True, vmem_limit_bytes=62 * 1024 * 1024
        ),
        cost_estimate=pl.CostEstimate(flops=2 * ROWS * 3 * M * W * 2 * W, bytes_accessed=6 << 20, transcendentals=0),
    )(low, high, margin_place, density_pattern, density_panel, margin_blocks[0])


def solution(mesh):
    return jax.shard_map(
        on_device,
        mesh=mesh,
        in_specs=(
            P("row", "col"),
            P("row", "col"),
            P("row", "col", None, None),
            P("row", "col", None),
            P("row", "col"),
        ),
        out_specs=P("row", "col"),
        check_vma=False,
    )
```

```python
import functools

import jax
import jax.numpy as jnp
from jax import lax
from jax.experimental import pallas as pl
from jax.experimental.pallas import tpu as pltpu
from jax.sharding import PartitionSpec as P

MESH = pl.DeviceIdType.MESH
NR = 24
NC = 32
W = 128
M = 8
LT = 3
RT = 4
ROWS = 512
CHUNKS = 4
DEEP = M * W // CHUNKS
H = W // 2


def spread(c):
    return c // 8, (c // 2) % 4, c % 2


def joined(x, y, k):
    return lax.rem(x + 4, 4) * 8 + lax.rem(y + 4, 4) * 2 + lax.rem(k + 2, 2)


def kernel(
    low, high, places, pattern, density, blocks, out,
    blk, a_own, a_ext, a_r1, a_r2, send, recv, relay, msend, mrecv, mrelay,
    acc, acc_x, b_own, b_ext, b_r1, b_r2,
    in_sem, d_send, d_recv, m_send, m_recv, y_send, y_recv, n_send, n_recv,
    a2_send, a2_recv, a1_send, a1_recv, b2_send, b2_recv, b1_send, b1_recv,
):
    r = lax.axis_index("row")
    c = lax.axis_index("col")
    x, y, k = spread(c)

    def at_offset(d, sign):
        dx, dy, dk = spread(d)
        return joined(x + sign * dx, y + sign * dy, k + dk)

    barrier = pltpu.get_barrier_semaphore()

    def greet(d, carry):
        pl.semaphore_signal(
            barrier, inc=1, device_id=(r, lax.rem(c + d, NC)), device_id_type=MESH
        )
        return carry

    lax.fori_loop(1, NC, greet, 0)
    near = r + 1 - 2 * lax.rem(r, 2)
    above = lax.rem(r + 2, NR)
    below = lax.rem(r + NR - 2, NR)
    pl.semaphore_signal(barrier, inc=1, device_id=(near, c), device_id_type=MESH)
    pl.semaphore_signal(barrier, inc=1, device_id=(above, c), device_id_type=MESH)

    own_first = (r + c) // NC
    ext_first = (r + lax.rem(c + NC - 2, NC) + 2) // NC

    def block_load():
        return pltpu.make_async_copy(blocks, blk, in_sem.at[0])

    def panel_load(first, place, sem, m):
        return pltpu.make_async_copy(
            density.at[:, pl.ds(pl.multiple_of((first + LT * m) * W, W), W)],
            place.at[:, m * W:(m + 1) * W],
            in_sem.at[sem + m],
        )

    block_load().start()
    for m in range(M):
        panel_load(ext_first, a_ext, 1, m).start()
    for m in range(M):
        panel_load(own_first, a_own, 1 + M, m).start()

    def pack(d):
        owner = at_offset(d, 1)
        one = low[owner]
        two = high[owner]
        first = jnp.where(two < 0, 0, one)
        second = jnp.maximum(two, 0)
        for slot, value in ((0, blk[first]), (1, blk[second])):
            send[d, 0, slot] = value[:H]
            send[d, 1, slot] = value[H:]
        first = jnp.where(two < 0, -1, places[0, first])
        second = jnp.where((two < 0) | (two == one), -1, places[0, second])
        msend[d, 0:1] = jnp.full((1, W), first, jnp.int32)
        msend[d, 1:2] = jnp.full((1, W), second, jnp.int32)

    def gate(first, place):
        def one(i, carry):
            rows = pl.ds(pl.multiple_of(i * W, W), W)
            for m in range(M):
                keep = pattern[i, first + LT * m] != 0
                value = place[rows, m * W:(m + 1) * W]
                place[rows, m * W:(m + 1) * W] = jnp.where(keep, value, jnp.zeros_like(value))
            return carry

        lax.fori_loop(0, ROWS // W, one, 0)

    block_load().wait()
    pl.semaphore_wait(barrier, NC + 1)

    def direct(d, h):
        return pltpu.make_async_remote_copy(
            send.at[d, h], recv.at[d, h], d_send.at[d, h], d_recv.at[d, h],
            device_id=(r, at_offset(d, 1)), device_id_type=MESH,
        )

    def direct_place(d):
        return pltpu.make_async_remote_copy(
            msend.at[d], mrecv.at[d], m_send.at[d], m_recv.at[d],
            device_id=(r, at_offset(d, 1)), device_id_type=MESH,
        )

    def offset_of(e, dy):
        return (e // 2) * 8 + dy * 2 + lax.rem(e, 2)

    def first_leg(e, h):
        d = offset_of(e, 2)
        return pltpu.make_async_remote_copy(
            send.at[d, h], relay.at[e, h], d_send.at[d, h], y_recv.at[e, h],
            device_id=(r, at_offset(offset_of(e, 1), 1)), device_id_type=MESH,
        )

    def first_place(e):
        d = offset_of(e, 2)
        return pltpu.make_async_remote_copy(
            msend.at[d], mrelay.at[e], m_send.at[d], n_recv.at[e],
            device_id=(r, at_offset(offset_of(e, 1), 1)), device_id_type=MESH,
        )

    def second_leg(e, h):
        d = offset_of(e, 2)
        return pltpu.make_async_remote_copy(
            relay.at[e, h], recv.at[d, h], y_send.at[e, h], d_recv.at[d, h],
            device_id=(r, joined(x, y + 1, k)), device_id_type=MESH,
        )

    def second_place(e):
        d = offset_of(e, 2)
        return pltpu.make_async_remote_copy(
            mrelay.at[e], mrecv.at[d], n_send.at[e], m_recv.at[d],
            device_id=(r, joined(x, y + 1, k)), device_id_type=MESH,
        )

    def panel_shift(i):
        rows = pl.ds(pl.multiple_of(i * W, W), W)
        return pltpu.make_async_remote_copy(
            a_ext.at[rows], a_r2.at[rows], a2_send.at[i], a2_recv.at[i],
            device_id=(r, lax.rem(c + NC - 2, NC)), device_id_type=MESH,
        )

    def panel_across(source, i):
        rows = pl.ds(pl.multiple_of(i * W, W), W)
        return pltpu.make_async_remote_copy(
            source.at[rows], a_r1.at[rows], a1_send.at[i], a1_recv.at[i],
            device_id=(r, c + 1 - 2 * k), device_id_type=MESH,
        )

    def send_first(e, carry):
        pack(offset_of(e, 2))
        first_place(e).start()
        first_leg(e, 0).start()
        pack(offset_of(e, 3))
        direct_place(offset_of(e, 3)).start()
        direct(offset_of(e, 3), 0).start()
        return carry

    lax.fori_loop(0, 8, send_first, 0)

    def send_next(e, carry):
        pack(offset_of(e, 1))
        direct_place(offset_of(e, 1)).start()
        direct(offset_of(e, 1), 0).start()
        pack(offset_of(e, 0))

        @pl.when(e > 0)
        def _():
            direct_place(offset_of(e, 0)).start()
            direct(offset_of(e, 0), 0).start()

        return carry

    lax.fori_loop(0, 8, send_next, 0)

    def send_far(e, carry):
        first_leg(e, 1).start()
        return carry

    lax.fori_loop(0, 8, send_far, 0)

    def send_second(e, carry):
        direct(offset_of(e, 3), 1).start()
        direct(offset_of(e, 1), 1).start()

        @pl.when(e > 0)
        def _():
            direct(offset_of(e, 0), 1).start()

        return carry

    lax.fori_loop(0, 8, send_second, 0)

    for m in range(M):
        panel_load(ext_first, a_ext, 1, m).wait()
    gate(ext_first, a_ext)

    recv[0] = send[0]
    mrecv[0] = msend[0]
    for m in range(M):
        panel_load(own_first, a_own, 1 + M, m).wait()
    gate(own_first, a_own)

    @pl.when(k == 1)
    def _():
        def one(i, carry):
            panel_across(a_own, i).start()
            return carry

        lax.fori_loop(0, CHUNKS, one, 0)

    def pass_on(e, carry):
        first_place(e).wait_recv()
        first_leg(e, 0).wait_recv()
        second_place(e).start()
        second_leg(e, 0).start()

        @pl.when(e % 2 == 1)
        def _():
            panel_shift(e // 2).start()

        return carry

    lax.fori_loop(0, 8, pass_on, 0)

    right_first = (r + c) // NR

    G = H // 8

    def add_pair(d, h):
        values = [recv[d, h, slot].astype(jnp.float32).reshape(G, 8, W) for slot in range(2)]
        places = [jnp.broadcast_to(mrecv[d, slot:slot + 1], (8, W)) for slot in range(2)]

        def into(sums, first):
            def one(m, carry):
                for q in range(2):
                    total = sums[2 * m + q, h * G:(h + 1) * G]
                    for slot in range(2):
                        hit = (places[slot] == 2 * first + 8 * m + q)[None]
                        total = total + jnp.where(hit, values[slot], 0.0)
                    sums[2 * m + q, h * G:(h + 1) * G] = total
                return carry

            lax.fori_loop(0, M, one, 0)

        into(acc, right_first)

        @pl.when(r < 2)
        def _():
            into(acc_x, right_first + 1)

    def take(d, h):
        if h == 0:
            direct_place(d).wait_recv()
        direct(d, h).wait_recv()
        add_pair(d, h)

    def clear(position, carry):
        acc[position] = jnp.zeros((W // 8, 8, W), jnp.float32)
        acc_x[position] = jnp.zeros((W // 8, 8, W), jnp.float32)
        return carry

    lax.fori_loop(0, 2 * M, clear, 0)
    odd = lax.rem(r, 2) == 1

    def down_two(ch, h):
        part = pl.ds(2 * ch, 2)
        return pltpu.make_async_remote_copy(
            b_ext.at[part, h], b_r2.at[part, h], b2_send.at[ch, h], b2_recv.at[ch, h],
            device_id=(below, c), device_id_type=MESH,
        )

    def beside(source, ch, h):
        part = pl.ds(2 * ch, 2)
        return pltpu.make_async_remote_copy(
            source.at[part, h], b_r1.at[part, h], b1_send.at[ch, h], b1_recv.at[ch, h],
            device_id=(near, c), device_id_type=MESH,
        )

    def finish(h):
        def one(ch, carry):
            for half in range(2):
                m = 2 * ch + half
                for q in range(2):
                    lanes = slice(q * W, (q + 1) * W)
                    value = acc[2 * m + q, h * G:(h + 1) * G].reshape(H, W).astype(jnp.bfloat16)
                    b_own[m, h, :, lanes] = value

                    @pl.when(r >= 2)
                    def _():
                        b_ext[m, h, :, lanes] = value

                    @pl.when(r < 2)
                    def _():
                        b_ext[m, h, :, lanes] = (
                            acc_x[2 * m + q, h * G:(h + 1) * G].reshape(H, W).astype(jnp.bfloat16)
                        )

            down_two(ch, h).start()

            @pl.when(odd)
            def _():
                beside(b_own, ch, h).start()

            return carry

        lax.fori_loop(0, CHUNKS, one, 0)

    def hand_on(ch, h):
        down_two(ch, h).wait_recv()

        @pl.when(jnp.logical_not(odd))
        def _():
            beside(b_r2, ch, h).start()

    def take_behind(e, carry, h):
        take(offset_of(e, 3), h)
        return carry

    def take_ahead(e, carry, h):
        if h == 0:
            first_leg(e, 1).wait_recv()
            second_leg(e, 1).start()
        take(offset_of(e, 1), h)

        @pl.when(e > 0)
        def _():
            take(offset_of(e, 0), h)

        return carry

    def take_far(e, carry, h):
        take(offset_of(e, 2), h)
        if h == 1:

            @pl.when(e % 2 == 1)
            def _():
                hand_on(e // 2, 0)

        return carry

    for h in range(2):
        add_pair(0, h)
        lax.fori_loop(0, 8, functools.partial(take_behind, h=h), 0)
        lax.fori_loop(0, 8, functools.partial(take_ahead, h=h), 0)
        lax.fori_loop(0, 8, functools.partial(take_far, h=h), 0)
        finish(h)

    def add_product(left, right, ch):
        depth = pl.ds(pl.multiple_of(ch * DEEP, DEEP), DEEP)
        piece = right[pl.ds(2 * ch, 2)].reshape(DEEP, 2 * W)
        out[...] += jnp.dot(left[:, depth], piece, preferred_element_type=jnp.float32)

    def panel_arrives(i, carry):
        panel_shift(i).wait_recv()

        @pl.when(k == 0)
        def _():
            panel_across(a_r2, i).start()

        return carry

    lax.fori_loop(0, CHUNKS, panel_arrives, 0)
    out[...] = jnp.zeros_like(out)

    def local_part(ch, carry):
        add_product(a_own, b_own, ch)
        return carry

    lax.fori_loop(0, CHUNKS, local_part, 0)

    def two_up(ch, carry):
        hand_on(ch, 1)
        add_product(a_r2, b_r2, ch)
        return carry

    lax.fori_loop(0, CHUNKS, two_up, 0)

    def across_arrives(i, carry):
        panel_across(a_own, i).wait_recv()
        return carry

    lax.fori_loop(0, CHUNKS, across_arrives, 0)

    def one_up(ch, carry):
        beside(b_own, ch, 0).wait_recv()
        beside(b_own, ch, 1).wait_recv()
        add_product(a_r1, b_r1, ch)
        return carry

    lax.fori_loop(0, CHUNKS, one_up, 0)

    def sent(d, carry):
        direct_place(d).wait_send()
        direct(d, 0).wait_send()
        direct(d, 1).wait_send()
        return carry

    lax.fori_loop(1, NC, sent, 0)

    def passed(e, carry):
        second_place(e).wait_send()
        second_leg(e, 0).wait_send()
        second_leg(e, 1).wait_send()
        return carry

    lax.fori_loop(0, 8, passed, 0)

    def rest(i, carry):
        panel_shift(i).wait_send()
        panel_across(a_own, i).wait_send()
        for h in range(2):
            down_two(i, h).wait_send()
            beside(b_own, i, h).wait_send()
        return carry

    lax.fori_loop(0, CHUNKS, rest, 0)


def on_device(density_panel, density_pattern, margin_blocks, margin_owner, margin_place):
    stack = margin_blocks.shape[1]
    owners = margin_owner[0, :, 0]
    index = jnp.arange(stack)[None, :]
    mine = owners[None, :] == jnp.arange(NC)[:, None]
    high = jnp.max(jnp.where(mine, index, -1), axis=1)
    low = jnp.min(jnp.where(mine, index, stack), axis=1)
    bf16, f32, i32 = jnp.bfloat16, jnp.float32, jnp.int32
    dma = pltpu.SemaphoreType.DMA
    return pl.pallas_call(
        kernel,
        out_shape=jax.ShapeDtypeStruct((ROWS, 2 * W), f32),
        in_specs=[
            pl.BlockSpec(memory_space=pltpu.SMEM),
            pl.BlockSpec(memory_space=pltpu.SMEM),
            pl.BlockSpec(memory_space=pltpu.SMEM),
            pl.BlockSpec(memory_space=pltpu.SMEM),
            pl.BlockSpec(memory_space=pl.ANY),
            pl.BlockSpec(memory_space=pl.ANY),
        ],
        out_specs=pl.BlockSpec(memory_space=pltpu.VMEM),
        scratch_shapes=[
            pltpu.VMEM((stack, W, W), bf16),
            pltpu.VMEM((ROWS, M * W), bf16),
            pltpu.VMEM((ROWS, M * W), bf16),
            pltpu.VMEM((ROWS, M * W), bf16),
            pltpu.VMEM((ROWS, M * W), bf16),
            pltpu.VMEM((NC, 2, 2, H, W), bf16),
            pltpu.VMEM((NC, 2, 2, H, W), bf16),
            pltpu.VMEM((8, 2, 2, H, W), bf16),
            pltpu.VMEM((NC, 2, W), i32),
            pltpu.VMEM((NC, 2, W), i32),
            pltpu.VMEM((8, 2, W), i32),
            pltpu.VMEM((2 * M, W // 8, 8, W), f32),
            pltpu.VMEM((2 * M, W // 8, 8, W), f32),
            pltpu.VMEM((M, 2, H, 2 * W), bf16),
            pltpu.VMEM((M, 2, H, 2 * W), bf16),
            pltpu.VMEM((M, 2, H, 2 * W), bf16),
            pltpu.VMEM((M, 2, H, 2 * W), bf16),
            dma((1 + 2 * M,)),
            dma((NC, 2)), dma((NC, 2)), dma((NC,)), dma((NC,)),
            dma((8, 2)), dma((8, 2)), dma((8,)), dma((8,)),
            dma((CHUNKS,)), dma((CHUNKS,)), dma((CHUNKS,)), dma((CHUNKS,)),
            dma((CHUNKS, 2)), dma((CHUNKS, 2)), dma((CHUNKS, 2)), dma((CHUNKS, 2)),
        ],
        compiler_params=pltpu.CompilerParams(
            collective_id=0, has_side_effects=True, vmem_limit_bytes=62 * 1024 * 1024
        ),
        cost_estimate=pl.CostEstimate(flops=2 * ROWS * 3 * M * W * 2 * W, bytes_accessed=6 << 20, transcendentals=0),
    )(low, high, margin_place, density_pattern, density_panel, margin_blocks[0])


def solution(mesh):
    return jax.shard_map(
        on_device,
        mesh=mesh,
        in_specs=(
            P("row", "col"),
            P("row", "col"),
            P("row", "col", None, None),
            P("row", "col", None),
            P("row", "col"),
        ),
        out_specs=P("row", "col"),
        check_vma=False,
    )
```
